512 devices in a mesh: wide: 128 (over y, z, core), narrow: 4 (over x).
Axes of the slice: x: 4, y: 8, z: 8, core: 2. Of those that a mesh axis runs over, the one named last changes fastest.
Arguments:
- iv_curves: bfloat16 [32768, 8192], P('wide', 'narrow'), may hold values from -25 to 25
- mean_curve: float32 [8192], P('narrow'), may hold values from -4 to 4
- loadings: bfloat16 [8192, 256], P('narrow'), may hold values from -0.0625 to 0.0625
- metrology: bfloat16 [32768, 2048], P('wide', 'narrow'), may hold values from -35 to 35
- dest_owner: int32 [32768], P('wide'), may hold values from 0 to 127, as said below
- dest_row: int32 [32768], P('wide'), may hold values from 0 to 255, as said below
Outputs:
- residual_msq: float32 [32768], P(('wide', 'narrow'))
- cross_z: float32 [256, 2048], P('wide', 'narrow')
The draws below stay inside these ranges and needn't reach their ends.
Inputs may be any that keep to these rules, and one draw needn't show every extreme that they name: Together with dest_row it names each wafer-order row dest_owner * 256 + dest_row exactly once, so every wide index owns the rows of 256 dies. The number of dies that wide index s sends to wide index o depends only on (o - s) modulo the wide axis's length; it is at most 4 and equals 4 for some offset. `dest_row`: see dest_owner.
All inputs are finite; a program needn't handle non-finite values.
Results may differ from the reference program's by a relative error of at most 0.0056.
Values may be sent and summed in bfloat16 or wider, within the bound.
A program may use at most 64 MiB of HBM per device.

```python
import math
import jax
import jax.numpy as jnp
from jax import lax

DIE_DEV = 256
F = 8192
K = 256
G = 2048
DIES = 32768
CAP = 4


def shuffle_rows(subkey):
    return jax.random.permutation(subkey, DIE_DEV).astype(jnp.int32)


def route_table(key):
    wide_count = DIES // DIE_DEV
    half_count = wide_count // 2
    key_list = jax.random.split(key, 4)
    lower_sizes = jax.random.randint(key_list[0], (half_count,), 0, CAP + 1).astype(jnp.int32)
    lower_sizes = lower_sizes.at[0].set(CAP)
    batch_sizes = jnp.concatenate([lower_sizes, CAP - lower_sizes])
    offsets = jax.random.permutation(key_list[1], wide_count).astype(jnp.int32)
    starts = jnp.cumsum(batch_sizes) - batch_sizes
    position = jnp.arange(DIE_DEV, dtype=jnp.int32)
    batch_index = jnp.sum((position[:, None] >= starts[None, :]).astype(jnp.int32), axis=1) - 1
    offset_of = offsets[batch_index]
    sources = jnp.arange(wide_count, dtype=jnp.int32)
    owner_at = (sources[:, None] + offset_of[None, :]) % wide_count
    row_order = jax.vmap(shuffle_rows)(jax.random.split(key_list[2], wide_count))
    row_at = row_order[owner_at, jnp.broadcast_to(position[None, :], owner_at.shape)]
    die_order = jax.vmap(shuffle_rows)(jax.random.split(key_list[3], wide_count))
    owner_grid = jnp.zeros((wide_count, DIE_DEV), jnp.int32).at[sources[:, None], die_order].set(owner_at)
    row_grid = jnp.zeros((wide_count, DIE_DEV), jnp.int32).at[sources[:, None], die_order].set(row_at)
    return (owner_grid.reshape(DIES), row_grid.reshape(DIES))


def draw_dest_owner(key, part):
    owner_list, row_list = route_table(key)
    return owner_list


def draw_dest_row(key, part):
    owner_list, row_list = route_table(key)
    return row_list


def draw_iv_curves(key, part):
    key = jax.random.fold_in(key, 7)
    key_list = jax.random.split(key, 4)
    row_place = jnp.arange(DIES, dtype=jnp.float32) / (DIES - 1)
    roughness = jax.random.uniform(key_list[0], (DIES,))
    row_scale = 0.3 * jnp.power(3.0, row_place) * jnp.power(10.0, 0.5 * roughness)
    col_scale = jnp.exp(jax.random.uniform(key_list[1], (F,), minval=math.log(0.5), maxval=math.log(2.0)))
    level_curve = jax.random.uniform(key_list[2], (F,), minval=-1.0, maxval=1.0)
    noise_part = jnp.clip(jax.random.normal(key_list[3], (DIES, F)), -4.0, 4.0)
    return (row_scale[:, None] * col_scale[None, :] * noise_part + (0.5 + row_place)[:, None] * level_curve[None, :]).astype(jnp.bfloat16)


def draw_metrology(key, part):
    key = jax.random.fold_in(key, 13)
    key_list = jax.random.split(key, 4)
    row_place = jnp.arange(DIES, dtype=jnp.float32) / (DIES - 1)
    roughness = jax.random.uniform(key_list[0], (DIES,))
    row_scale = 0.2 * jnp.power(3.0, row_place) * jnp.power(10.0, 0.5 * roughness)
    col_scale = jnp.exp(jax.random.uniform(key_list[1], (G,), minval=math.log(0.3), maxval=math.log(3.0)))
    offset_curve = jax.random.uniform(key_list[2], (G,), minval=-2.0, maxval=2.0)
    noise_part = jnp.clip(jax.random.normal(key_list[3], (DIES, G)), -4.0, 4.0)
    return (row_scale[:, None] * col_scale[None, :] * noise_part + (1.0 + 2.0 * row_place)[:, None] * offset_curve[None, :]).astype(jnp.bfloat16)


def steps_of(own_key, shape, pieces, least, largest):
    gain = 1.0
    for dim, parts in pieces:
        draws = jax.random.uniform(jax.random.fold_in(jax.random.fold_in(own_key, 6), dim), (parts,), jnp.float32, least / len(pieces), largest / len(pieces))
        gain = gain * jnp.repeat(jnp.exp(draws), shape[dim] // parts).reshape((-1,) + (1,) * (len(shape) - 1 - dim))
    return gain


def scatter_about(own_key, dims, scale, limit, cuts=(), kind=jnp.bfloat16):
    entries = scale * jax.random.normal(own_key, dims, jnp.float32)
    if cuts:
        entries = entries * steps_of(own_key, dims, cuts, -0.22, 0.18)
    return jnp.clip(entries, -limit, limit).astype(kind)


def setup_inputs(seed: int = 0) -> dict:
    splits = jax.random.split(jax.random.key(seed), 7)
    return {
        "iv_curves": draw_iv_curves(jax.random.fold_in(splits[6], 71), 0),
        "mean_curve": scatter_about(splits[1], (F,), 1.0, 4.0, ((0, 4),), jnp.float32),
        "loadings": scatter_about(splits[2], (F, K), F ** -0.5, 0.0625, ((0, 4),)),
        "metrology": draw_metrology(jax.random.fold_in(splits[6], 71), 0),
        "dest_owner": draw_dest_owner(jax.random.fold_in(splits[6], 71), 0),
        "dest_row": draw_dest_row(jax.random.fold_in(splits[6], 71), 0),
    }


EPSILON = 1e-05

def project_block(curve_block, mean_curve, loadings):
    centered = (curve_block.astype(jnp.float32) - mean_curve[None, :]).astype(jnp.bfloat16)
    scores = jnp.dot(centered, loadings, preferred_element_type=jnp.float32)
    score_bf = scores.astype(jnp.bfloat16)
    rebuilt = lax.dot_general(score_bf, loadings, (((1,), (1,)), ((), ())), preferred_element_type=jnp.float32)
    residue = centered.astype(jnp.float32) - rebuilt
    return (scores, lax.optimization_barrier(jnp.sum(residue * residue, axis=1)) / F)

def standardize(values):
    center = lax.optimization_barrier(jnp.sum(values, axis=0)) / DIES
    scaling = lax.rsqrt(lax.optimization_barrier(jnp.sum(values * values, axis=0)) / DIES - center * center + EPSILON)
    return ((values - center) * scaling).astype(jnp.bfloat16)

def reference(iv_curves, mean_curve, loadings, metrology, dest_owner, dest_row):
    blocks = iv_curves.reshape(DIES // DIE_DEV, DIE_DEV, F)

    def one_block(curve_block):
        return project_block(curve_block, mean_curve, loadings)
    scores, residual_msq = lax.map(one_block, blocks)
    scores = scores.reshape(DIES, K)
    residual_msq = residual_msq.reshape(DIES)
    score_z = standardize(scores)
    target = (dest_owner * DIE_DEV + dest_row).astype(jnp.int32)
    wafer_z = jnp.zeros((DIES, K), jnp.bfloat16).at[target].set(score_z)
    metro_z = standardize(metrology.astype(jnp.float32))
    cross_z = lax.dot_general(wafer_z, metro_z, (((0,), (0,)), ((), ())), preferred_element_type=jnp.float32) * (1.0 / math.sqrt(DIES))
    return (residual_msq, cross_z)
```

```python
import functools
import math

import jax
import jax.numpy as jnp
from jax import lax
from jax.experimental import pallas as pl
from jax.experimental.pallas import tpu as pltpu
from jax.sharding import PartitionSpec as P

EPSILON = 1e-05
MESH = pl.DeviceIdType.MESH
F32 = jnp.float32
BF16 = jnp.bfloat16

NY, NZ, NC, NX = 8, 8, 2, 4
CHIPS = NY * NZ
GROUP = NC * NX
DIES_DEV = 256
FEAT = 2048
COMP = 256
SLICE = COMP // GROUP
METRO = 512
TOTAL = DIES_DEV * CHIPS * NC
CHUNKS = 4
FAR = (4, 3, 5, 2, 6, 1, 7)
(S_ROUTE, S_SCORE, S_MET_X, S_MET_C, S_M1, S_M2, S_M3, S_R1, S_R2, S_CHIP, S_BACK, S_RES, S_OUT) = range(13)
N_SEM = 13


def body(
    iv_hbm, mean_hbm, load_hbm, met_hbm, own_hbm, row_hbm,
    res_out, cross_out,
    iv_v, mean_v, load_v, cen_v, pt_v, met_v, mz_v, route_v,
    asnd, arcv, st_v, bsnd, brcv, oh_v, ohr_v,
    csnd, crcv, dsnd, drcv,
    m1snd, m1rcv, m2snd, m2rcv, m3snd, m3rcv,
    r1snd, r1rcv, r2snd, r2rcv, esnd, ercv,
    ld_sem, ssem, rsem, plane_sem,
):
    w = lax.axis_index("wide")
    n = lax.axis_index("narrow")
    y, z, c = w // 16, (w // 2) % 8, w % 2
    me8 = c * NX + n
    chip = y * NZ + z

    def dev(yy, zz, cc, nn):
        return (yy * 16 + zz * 2 + cc, nn)

    def send(k, src, dst, device):
        pltpu.make_async_remote_copy(
            src_ref=src, dst_ref=dst, send_sem=ssem.at[k], recv_sem=rsem.at[k],
            device_id=device, device_id_type=MESH,
        ).start()

    def got(k, ref):
        pltpu.make_async_copy(ref, ref, rsem.at[k]).wait()

    def sent(k, ref):
        pltpu.make_async_copy(ref, ref, ssem.at[k]).wait()

    group_peers = [((c + dc) % NC, (n + dn) % NX) for dn in (2, 1, 3, 0) for dc in (0, 1) if (dc, dn) != (0, 0)]
    z_peers = [(z + d) % NZ for d in FAR]
    y_peers = [(y + d) % NY for d in FAR]

    step = FEAT // CHUNKS
    loads = []
    for j in range(CHUNKS):
        span = pl.ds(j * step, step)
        loads.append((
            pltpu.make_async_copy(iv_hbm.at[:, span], iv_v.at[:, span], ld_sem.at[2 * j]),
            pltpu.make_async_copy(load_hbm.at[span], load_v.at[span], ld_sem.at[2 * j + 1]),
        ))
    mean_load = pltpu.make_async_copy(mean_hbm, mean_v, ld_sem.at[2 * CHUNKS])
    met_load = pltpu.make_async_copy(met_hbm, met_v.at[me8], ld_sem.at[2 * CHUNKS + 1])
    own_load = pltpu.make_async_copy(own_hbm, route_v.at[c, 0], ld_sem.at[2 * CHUNKS + 2])
    row_load = pltpu.make_async_copy(row_hbm, route_v.at[c, 1], ld_sem.at[2 * CHUNKS + 3])
    mean_load.start()
    for a, b in loads:
        a.start()
        b.start()
    met_load.start()
    own_load.start()
    row_load.start()

    barrier = pltpu.get_barrier_semaphore()
    for zz in z_peers:
        pl.semaphore_signal(barrier, inc=1, device_id=dev(y, zz, c, n), device_id_type=MESH)
    for yy in y_peers:
        pl.semaphore_signal(barrier, inc=1, device_id=dev(yy, z, c, n), device_id_type=MESH)
    for cc, nn in group_peers:
        pl.semaphore_signal(barrier, inc=1, device_id=dev(y, z, cc, nn), device_id_type=MESH)

    mean_load.wait()
    part = jnp.zeros((DIES_DEV, COMP), F32)
    for j, (a, b) in enumerate(loads):
        a.wait()
        b.wait()
        span = pl.ds(j * step, step)
        cen = (iv_v[:, span].astype(F32) - mean_v[:, span]).astype(BF16)
        cen_v[:, span] = cen
        part = part + jnp.dot(cen, load_v[span, :], preferred_element_type=F32)
    pt_v[...] = part.T
    for q in range(GROUP):
        for yy in range(NY):
            asnd[q, 4 * yy:4 * yy + 4, :] = pt_v[pl.ds(32 * yy + 4 * ((q + yy) % NZ), 4), :]

    met_load.wait()
    met = met_v[me8].astype(F32)
    tot = jnp.sum(met, axis=0, keepdims=True)
    sq = jnp.sum(met * met, axis=0, keepdims=True)
    for t in range(4):
        m1snd[t:t + 1, :] = tot[:, 128 * t:128 * t + 128]
        m1snd[4 + t:5 + t, :] = sq[:, 128 * t:128 * t + 128]
    own_load.wait()
    row_load.wait()

    pl.semaphore_wait(barrier, len(z_peers) + len(y_peers) + len(group_peers))

    for cc, nn in group_peers:
        q = cc * NX + nn
        send(S_SCORE, asnd.at[q], arcv.at[me8], dev(y, z, cc, nn))
    send(S_ROUTE, route_v.at[c], route_v.at[c], dev(y, z, 1 - c, n))
    for zz in z_peers:
        send(S_M1, m1snd, m1rcv.at[z], dev(y, zz, c, n))
    for yy in y_peers:
        pl.semaphore_signal(plane_sem, inc=1, device_id=dev(yy, z, c, n), device_id_type=MESH)
    for dn in (2, 1, 3):
        send(S_MET_X, met_v.at[me8], met_v.at[me8], dev(y, z, c, (n + dn) % NX))
    send(S_MET_C, met_v.at[me8], met_v.at[me8], dev(y, z, 1 - c, n))
    arcv[me8] = asnd[me8]
    m1rcv[z] = m1snd[...]

    got(S_ROUTE, route_v.at[0])
    targets, lanes, zds, rows1 = [], [], [], []
    for cs in range(NC):
        owner = jnp.concatenate([route_v[cs, 0, 0:1, :], route_v[cs, 0, 1:2, :]], axis=1)
        row = jnp.concatenate([route_v[cs, 1, 0:1, :], route_v[cs, 1, 1:2, :]], axis=1)
        wide_o = jnp.broadcast_to(owner.astype(F32), (DIES_DEV, DIES_DEV))
        before = lax.broadcasted_iota(jnp.int32, (DIES_DEV, DIES_DEV), 0) < lax.broadcasted_iota(
            jnp.int32, (DIES_DEV, DIES_DEV), 1)
        same = jnp.where((wide_o.T == wide_o) & before, 1.0, 0.0)
        rank = jnp.sum(same, axis=0, keepdims=True).astype(jnp.int32)
        oc = owner & 1
        och = owner >> 1
        r = 2 * oc + cs
        targets.append(rank * 256 + r * 64 + och)
        lanes.append((och >> 3) * 16 + r * 4 + rank)
        zds.append(och & 7)
        rows1.append((row + 1).astype(F32))
    target = jnp.concatenate(targets, axis=1)
    lane = jnp.concatenate(lanes, axis=1)
    zd = jnp.concatenate(zds, axis=1)
    row1 = jnp.concatenate(rows1, axis=1)
    two = NC * DIES_DEV
    left = jnp.where(lax.broadcasted_iota(jnp.int32, (8, two), 0) == zd, row1, 0.0).astype(BF16)
    right = jnp.where(lax.broadcasted_iota(jnp.int32, (128, two), 0) == lane, 1.0, 0.0).astype(BF16)
    table = lax.dot_general(left, right, (((1,), (1,)), ((), ())), preferred_element_type=F32)
    for zz in range(NZ):
        r1snd[zz] = table[zz:zz + 1, :]
    for zz in z_peers:
        send(S_R1, r1snd.at[zz], r1rcv.at[z], dev(y, zz, c, n))
    r1rcv[z] = r1snd[z]
    for l in range(4):
        oh_v[256 * l:256 * l + 256, :] = jnp.where(
            lax.broadcasted_iota(jnp.int32, (256, two), 0) + 256 * l == target, 1.0, 0.0).astype(BF16)

    got(S_M1, m1rcv.at[pl.ds(0, 7)])
    m2snd[...] = jnp.sum(m1rcv[...], axis=0)
    for yy in y_peers:
        send(S_M2, m2snd, m2rcv.at[y], dev(yy, z, c, n))
    m2rcv[y] = m2snd[...]

    got(S_SCORE, arcv.at[pl.ds(0, 7)])
    halves = []
    for cs in range(NC):
        half = (arcv[4 * cs] + arcv[4 * cs + 1]) + (arcv[4 * cs + 2] + arcv[4 * cs + 3])
        for t in range(2):
            st_v[2 * cs + t] = half[:, 128 * t:128 * t + 128]
        halves.append(half)
    tiles = []
    for t in range(4):
        ordered = jnp.concatenate([st_v[t, pl.ds(0, 16, 2), :], st_v[t, pl.ds(1, 16, 2), :]], axis=0)
        tiles.append(jnp.concatenate([ordered] * 4, axis=0).T)
    s4 = jnp.concatenate(tiles, axis=0)
    hi = s4.astype(BF16)
    lo = (s4 - hi.astype(F32)).astype(BF16)
    packed = jnp.dot(oh_v[...], jnp.concatenate([hi, lo], axis=1), preferred_element_type=F32)
    lane_group = lax.broadcasted_iota(jnp.int32, (256, 128), 1) // SLICE
    slots = jnp.zeros((256, 128), F32)
    for l in range(4):
        piece = packed[256 * l:256 * l + 256, :]
        slots = jnp.where(lane_group == l, piece[:, :128] + piece[:, 128:], slots)
    for r in range(4):
        csnd[:, r, :] = slots[64 * r:64 * r + 64, :]
    first = jnp.sum(s4, axis=0, keepdims=True)
    second = jnp.sum(s4 * s4, axis=0, keepdims=True)
    stat = jnp.where(lax.broadcasted_iota(jnp.int32, (1, 128), 1) < SLICE, first, second)
    csnd[:, 4, :] = jnp.broadcast_to(stat, (CHIPS, 128))

    pl.semaphore_wait(plane_sem, len(y_peers))
    order = sorted(range(1, CHIPS), key=lambda j: -(min(j // 8, 8 - j // 8) + min(j % 8, 8 - j % 8)))
    for j in order:
        yy, zz = (y + j // 8) % NY, (z + j % 8) % NZ
        send(S_CHIP, csnd.at[yy * NZ + zz], crcv.at[chip], dev(yy, zz, c, n))
    crcv[chip] = csnd[chip]

    for cs in range(NC):
        bsnd[cs] = halves[cs].astype(BF16)
    for cc, nn in group_peers:
        send(S_BACK, bsnd.at[cc], brcv.at[me8], dev(y, z, cc, nn))
    brcv[me8] = bsnd[c]

    got(S_R1, r1rcv.at[pl.ds(0, 7)])
    here = r1rcv[:, 0, :]
    for yy in range(NY):
        r2snd[yy] = here if yy == 0 else pltpu.roll(here, 128 - 16 * yy, 1)
    for yy in y_peers:
        send(S_R2, r2snd.at[yy], r2rcv.at[y], dev(yy, z, c, n))
    r2rcv[y] = r2snd[y]

    got(S_M2, m2rcv.at[pl.ds(0, 7)])
    m3snd[...] = jnp.sum(m2rcv[...], axis=0)
    for cc, nn in group_peers:
        send(S_M3, m3snd, m3rcv.at[me8], dev(y, z, cc, nn))
    m3rcv[me8] = m3snd[...]

    got(S_MET_X, met_v.at[pl.ds(0, 3)])
    for dn in (1, 2, 3):
        blk = c * NX + (n + dn) % NX
        send(S_MET_C, met_v.at[blk], met_v.at[blk], dev(y, z, 1 - c, n))

    got(S_R2, r2rcv.at[pl.ds(0, 7)])
    rr = r2rcv[...].reshape(CHIPS, 128).astype(jnp.int32)
    spot = lax.broadcasted_iota(jnp.int32, (CHIPS, DIES_DEV), 1) + 1
    for cp in range(NC):
        for l in range(4):
            for cs in range(NC):
                s16 = (2 * cp + cs) * 4 + l
                ohr_v[cp, pl.ds(l * 128 + cs * 64, 64), :] = jnp.where(
                    rr[:, s16:s16 + 1] == spot, 1.0, 0.0).astype(BF16)

    got(S_M3, m3rcv.at[pl.ds(0, 7)])
    got(S_MET_C, met_v.at[pl.ds(0, 4)])
    for nn in range(NX):
        both = m3rcv[nn] + m3rcv[NX + nn]
        center = both[0:4, :] / TOTAL
        scaling = lax.rsqrt(both[4:8, :] / TOTAL - center * center + EPSILON)
        for cs in range(NC):
            blk = cs * NX + nn
            for t in range(4):
                span = slice(128 * t, 128 * t + 128)
                mz_v[blk, :, span] = (
                    (met_v[blk, :, span].astype(F32) - center[t:t + 1, :]) * scaling[t:t + 1, :]
                ).astype(BF16)

    got(S_CHIP, crcv.at[pl.ds(0, 63)])
    stat = jnp.sum(crcv[:, 4, :], axis=0, keepdims=True)
    lg = lax.broadcasted_iota(jnp.int32, (1, 128), 1) // SLICE
    s1 = jnp.where(lg == 0, stat, 0.0)
    s2 = jnp.where(lg == 1, stat, 0.0)
    s1 = s1 + pltpu.roll(s1, 32, 1)
    s1 = s1 + pltpu.roll(s1, 64, 1)
    s2 = s2 + pltpu.roll(s2, 32, 1)
    s2 = s2 + pltpu.roll(s2, 64, 1)
    center = s1 / TOTAL
    scaling = lax.rsqrt(s2 / TOTAL - center * center + EPSILON)
    zf = jnp.concatenate([(crcv[:, r, :] - center) * scaling for r in range(4)], axis=0)
    zt = zf.T.astype(BF16)
    placed = []
    for cp in range(NC):
        lhs = jnp.concatenate([zt[32 * l:32 * l + 32, 128 * cp:128 * cp + 128] for l in range(4)], axis=1)
        placed.append(jnp.dot(lhs, ohr_v[cp], preferred_element_type=F32).astype(BF16))
    for nn in range(NX):
        cross = jnp.dot(placed[0], mz_v[nn], preferred_element_type=F32) + jnp.dot(
            placed[1], mz_v[NX + nn], preferred_element_type=F32)
        for t in range(4):
            for kk in range(2):
                dsnd[pl.ds(nn * 8 + t * 2 + kk, 16, 32), :] = cross[16 * kk:16 * kk + 16, 128 * t:128 * t + 128]

    mine = (c * NX + n + y) % NZ == z
    for dy in FAR + (0,):
        yy = (y + dy) % NY
        zz = (me8 + yy) % NZ
        for dc, dn in ((0, 2), (1, 2), (0, 1), (1, 1), (0, 3), (1, 3), (1, 0), (0, 0)):
            cc, nn = (c + dc) % NC, (n + dn) % NX
            src = dsnd.at[pl.ds(pl.multiple_of(((yy * 2 + cc) * 4 + nn) * 8, 8), 8), :]
            if (dy, dc, dn) == (0, 0, 0):
                @pl.when(jnp.logical_not(mine))
                def _():
                    send(S_OUT, src, drcv.at[chip], dev(yy, zz, cc, nn))

                @pl.when(mine)
                def _():
                    pltpu.make_async_copy(src, drcv.at[chip], rsem.at[S_OUT]).start()
            else:
                send(S_OUT, src, drcv.at[chip], dev(yy, zz, cc, nn))

    got(S_BACK, brcv.at[pl.ds(0, 7)])
    slot_k = lax.broadcasted_iota(jnp.int32, (COMP, COMP), 1)
    q_of, y_of, rest = slot_k // 32, (slot_k // 4) % 8, slot_k % 4
    natural = 32 * y_of + 4 * ((q_of + y_of) % 8) + rest
    perm = jnp.where(lax.broadcasted_iota(jnp.int32, (COMP, COMP), 0) == natural, 1.0, 0.0).astype(BF16)
    score_t = jnp.dot(perm, brcv[...].reshape(COMP, DIES_DEV), preferred_element_type=F32)
    score = score_t.T.astype(BF16)
    acc = jnp.zeros((DIES_DEV, 128), F32)
    for j in range(CHUNKS):
        span = pl.ds(j * step, step)
        rebuilt = lax.dot_general(
            score, load_v[span, :], (((1,), (1,)), ((), ())), preferred_element_type=F32)
        residue = cen_v[:, span].astype(F32) - rebuilt
        residue = residue * residue
        for t in range(step // 128):
            acc = acc + residue[:, 128 * t:128 * t + 128]
    line = jnp.sum(acc.T, axis=0, keepdims=True) / (FEAT * NX)
    esnd[0:1, :] = line[:, :128]
    esnd[1:2, :] = line[:, 128:]
    for dn in (2, 1, 3):
        send(S_RES, esnd, ercv.at[n], dev(y, z, c, (n + dn) % NX))
    ercv[n] = esnd[...]
    got(S_RES, ercv.at[pl.ds(0, 3)])
    total = (ercv[0] + ercv[1]) + (ercv[2] + ercv[3])
    pick = jnp.where(n >= 2, total[1:2, :], total[0:1, :])
    res_out[...] = jnp.where(n % 2 == 1, pick[:, 64:], pick[:, :64])

    got(S_OUT, drcv)
    out = jnp.sum(drcv[...], axis=0) * (1.0 / math.sqrt(TOTAL))
    for t in range(4):
        cross_out[:, 128 * t:128 * t + 128] = out[2 * t:2 * t + 2, :]

    sent(S_SCORE, asnd.at[pl.ds(0, 7)])
    sent(S_ROUTE, route_v.at[0])
    for _ in range(7):
        sent(S_M1, m1snd)
        sent(S_M2, m2snd)
        sent(S_M3, m3snd)
    sent(S_MET_X, met_v.at[pl.ds(0, 3)])
    sent(S_MET_C, met_v.at[pl.ds(0, 4)])
    sent(S_R1, r1snd.at[pl.ds(0, 7)])
    sent(S_R2, r2snd.at[pl.ds(0, 7)])
    sent(S_CHIP, csnd.at[pl.ds(0, 63)])
    sent(S_BACK, brcv.at[pl.ds(0, 7)])
    sent(S_RES, ercv.at[pl.ds(0, 3)])
    sent(S_OUT, drcv.at[pl.ds(0, 63)])

    @pl.when(jnp.logical_not(mine))
    def _():
        sent(S_OUT, drcv.at[0])


def shards(iv_curves, mean_curve, loadings, metrology, dest_owner, dest_row):
    any_spec = pl.BlockSpec(memory_space=pl.ANY)
    vmem_spec = pl.BlockSpec(memory_space=pltpu.VMEM)
    scratch = [
        pltpu.VMEM((DIES_DEV, FEAT), BF16),
        pltpu.VMEM((1, FEAT), F32),
        pltpu.VMEM((FEAT, COMP), BF16),
        pltpu.VMEM((DIES_DEV, FEAT), BF16),
        pltpu.VMEM((COMP, DIES_DEV), F32),
        pltpu.VMEM((GROUP, DIES_DEV, METRO), BF16),
        pltpu.VMEM((GROUP, DIES_DEV, METRO), BF16),
        pltpu.VMEM((NC, 2, 2, 128), jnp.int32),
        pltpu.VMEM((GROUP, SLICE, DIES_DEV), F32),
        pltpu.VMEM((GROUP, SLICE, DIES_DEV), F32),
        pltpu.VMEM((4, SLICE, 128), F32),
        pltpu.VMEM((NC, SLICE, DIES_DEV), BF16),
        pltpu.VMEM((GROUP, SLICE, DIES_DEV), BF16),
        pltpu.VMEM((1024, NC * DIES_DEV), BF16),
        pltpu.VMEM((NC, 512, DIES_DEV), BF16),
        pltpu.VMEM((CHIPS, 5, 128), F32),
        pltpu.VMEM((CHIPS, 5, 128), F32),
        pltpu.VMEM((CHIPS * 8, 128), F32),
        pltpu.VMEM((CHIPS, 8, 128), F32),
        pltpu.VMEM((8, 128), F32),
        pltpu.VMEM((NZ, 8, 128), F32),
        pltpu.VMEM((8, 128), F32),
        pltpu.VMEM((NY, 8, 128), F32),
        pltpu.VMEM((8, 128), F32),
        pltpu.VMEM((GROUP, 8, 128), F32),
        pltpu.VMEM((NZ, 1, 128), F32),
        pltpu.VMEM((NZ, 1, 128), F32),
        pltpu.VMEM((NY, 8, 128), F32),
        pltpu.VMEM((NY, 8, 128), F32),
        pltpu.VMEM((2, 128), F32),
        pltpu.VMEM((NX, 2, 128), F32),
        pltpu.SemaphoreType.DMA((2 * CHUNKS + 4,)),
        pltpu.SemaphoreType.DMA((N_SEM,)),
        pltpu.SemaphoreType.DMA((N_SEM,)),
        pltpu.SemaphoreType.REGULAR,
    ]
    residual, cross = pl.pallas_call(
        body,
        out_shape=(
            jax.ShapeDtypeStruct((1, DIES_DEV // NX), F32),
            jax.ShapeDtypeStruct((2, METRO), F32),
        ),
        in_specs=[any_spec] * 6,
        out_specs=(vmem_spec, vmem_spec),
        scratch_shapes=scratch,
        compiler_params=pltpu.CompilerParams(
            collective_id=1, has_side_effects=True, vmem_limit_bytes=40 * 2**20),
        cost_estimate=pl.CostEstimate(flops=10**9, bytes_accessed=3 * 10**6, transcendentals=0),
    )(
        iv_curves,
        mean_curve.reshape(1, FEAT),
        loadings,
        metrology,
        dest_owner.reshape(2, 128),
        dest_row.reshape(2, 128),
    )
    return residual.reshape(DIES_DEV // NX), cross


def solution(mesh):
    in_specs = (
        P("wide", "narrow"),
        P("narrow"),
        P("narrow", None),
        P("wide", "narrow"),
        P("wide"),
        P("wide"),
    )
    out_specs = (P(("wide", "narrow")), P("wide", "narrow"))
    return jax.shard_map(shards, mesh=mesh, in_specs=in_specs, out_specs=out_specs, check_vma=False)
```

```python
import functools
import math

import jax
import jax.numpy as jnp
from jax import lax
from jax.experimental import pallas as pl
from jax.experimental.pallas import tpu as pltpu
from jax.sharding import PartitionSpec as P

EPSILON = 1e-05
MESH = pl.DeviceIdType.MESH
F32 = jnp.float32
BF16 = jnp.bfloat16

NY, NZ, NC, NX = 8, 8, 2, 4
CHIPS = NY * NZ
GROUP = NC * NX
DIES_DEV = 256
FEAT = 2048
COMP = 256
SLICE = COMP // GROUP
METRO = 512
TOTAL = DIES_DEV * CHIPS * NC
CHUNKS = 4
FAR = (4, 3, 5, 2, 6, 1, 7)
(S_ROUTE, S_SCORE, S_MET, S_M1, S_M2, S_M3, S_R1, S_R2, S_CHIP, S_PLACED, S_BACK, S_RES, S_OUT) = range(13)
N_SEM = 13


def body(
    iv_hbm, mean_hbm, load_hbm, met_hbm, own_hbm, row_hbm,
    res_out, cross_out,
    iv_v, mean_v, load_v, cen_v, pt_v, met_v, mz_v, route_v,
    asnd, arcv, bsnd, brcv, oh_v, ohr_v,
    csnd, crcv, placed_v, dsnd, drcv,
    m1snd, m1rcv, m2snd, m2rcv, m3snd, m3rcv,
    r1snd, r1rcv, r2snd, r2rcv, esnd, ercv,
    ld_sem, ssem, rsem, plane_sem,
):
    w = lax.axis_index("wide")
    n = lax.axis_index("narrow")
    y, z, c = w // 16, (w // 2) % 8, w % 2
    me8 = c * NX + n
    chip = y * NZ + z

    def dev(yy, zz, cc, nn):
        return (yy * 16 + zz * 2 + cc, nn)

    def send(k, src, dst, device):
        pltpu.make_async_remote_copy(
            src_ref=src, dst_ref=dst, send_sem=ssem.at[k], recv_sem=rsem.at[k],
            device_id=device, device_id_type=MESH,
        ).start()

    def got(k, ref):
        pltpu.make_async_copy(ref, ref, rsem.at[k]).wait()

    def sent(k, ref):
        pltpu.make_async_copy(ref, ref, ssem.at[k]).wait()

    group_peers = [((c + dc) % NC, (n + dn) % NX) for dn in (2, 1, 3, 0) for dc in (0, 1) if (dc, dn) != (0, 0)]
    z_peers = [(z + d) % NZ for d in FAR]
    y_peers = [(y + d) % NY for d in FAR]

    step = FEAT // CHUNKS
    loads = []
    for j in range(CHUNKS):
        span = pl.ds(j * step, step)
        loads.append((
            pltpu.make_async_copy(iv_hbm.at[:, span], iv_v.at[:, span], ld_sem.at[2 * j]),
            pltpu.make_async_copy(load_hbm.at[span], load_v.at[span], ld_sem.at[2 * j + 1]),
        ))
    mean_load = pltpu.make_async_copy(mean_hbm, mean_v, ld_sem.at[2 * CHUNKS])
    met_load = pltpu.make_async_copy(met_hbm, met_v.at[c], ld_sem.at[2 * CHUNKS + 1])
    own_load = pltpu.make_async_copy(own_hbm, route_v.at[c, 0], ld_sem.at[2 * CHUNKS + 2])
    row_load = pltpu.make_async_copy(row_hbm, route_v.at[c, 1], ld_sem.at[2 * CHUNKS + 3])
    mean_load.start()
    for a, b in loads:
        a.start()
        b.start()
    met_load.start()
    own_load.start()
    row_load.start()

    barrier = pltpu.get_barrier_semaphore()
    for zz in z_peers:
        pl.semaphore_signal(barrier, inc=1, device_id=dev(y, zz, c, n), device_id_type=MESH)
    for yy in y_peers:
        pl.semaphore_signal(barrier, inc=1, device_id=dev(yy, z, c, n), device_id_type=MESH)
    for cc, nn in group_peers:
        pl.semaphore_signal(barrier, inc=1, device_id=dev(y, z, cc, nn), device_id_type=MESH)

    mean_load.wait()
    part = jnp.zeros((DIES_DEV, COMP), F32)
    for j, (a, b) in enumerate(loads):
        a.wait()
        b.wait()
        span = pl.ds(j * step, step)
        cen = (iv_v[:, span].astype(F32) - mean_v[:, span]).astype(BF16)
        cen_v[:, span] = cen
        part = part + jnp.dot(cen, load_v[span, :], preferred_element_type=F32)
    part_t = part.T
    for t in range(2):
        pt_v[t] = part_t[:, 128 * t:128 * t + 128]
    for cc in range(NC):
        for nn in range(NX):
            for kk in range(2):
                for t in range(2):
                    asnd[cc * NX + nn, 16 * kk:16 * kk + 16, 128 * t:128 * t + 128] = pt_v[
                        t, pl.ds(64 * nn + 2 * cc + kk, 16, 4), :]

    met_load.wait()
    met = met_v[c].astype(F32)
    tot = jnp.sum(met, axis=0, keepdims=True)
    sq = jnp.sum(met * met, axis=0, keepdims=True)
    for t in range(4):
        m1snd[t:t + 1, :] = tot[:, 128 * t:128 * t + 128]
        m1snd[4 + t:5 + t, :] = sq[:, 128 * t:128 * t + 128]
    own_load.wait()
    row_load.wait()

    pl.semaphore_wait(barrier, len(z_peers) + len(y_peers) + len(group_peers))

    for cc, nn in group_peers:
        q = cc * NX + nn
        send(S_SCORE, asnd.at[q], arcv.at[me8], dev(y, z, cc, nn))
    send(S_ROUTE, route_v.at[c], route_v.at[c], dev(y, z, 1 - c, n))
    for zz in z_peers:
        send(S_M1, m1snd, m1rcv.at[z], dev(y, zz, c, n))
    for yy in y_peers:
        pl.semaphore_signal(plane_sem, inc=1, device_id=dev(yy, z, c, n), device_id_type=MESH)
    send(S_MET, met_v.at[c], met_v.at[c], dev(y, z, 1 - c, n))
    arcv[me8] = asnd[me8]
    m1rcv[z] = m1snd[...]

    got(S_ROUTE, route_v.at[0])
    targets, lanes, zds, rows1 = [], [], [], []
    for cs in range(NC):
        owner = jnp.concatenate([route_v[cs, 0, 0:1, :], route_v[cs, 0, 1:2, :]], axis=1)
        row = jnp.concatenate([route_v[cs, 1, 0:1, :], route_v[cs, 1, 1:2, :]], axis=1)
        wide_o = jnp.broadcast_to(owner.astype(F32), (DIES_DEV, DIES_DEV))
        before = lax.broadcasted_iota(jnp.int32, (DIES_DEV, DIES_DEV), 0) < lax.broadcasted_iota(
            jnp.int32, (DIES_DEV, DIES_DEV), 1)
        same = jnp.where((wide_o.T == wide_o) & before, 1.0, 0.0)
        rank = jnp.sum(same, axis=0, keepdims=True).astype(jnp.int32)
        oc = owner & 1
        och = owner >> 1
        r = 2 * oc + cs
        targets.append(rank * 256 + r * 64 + och)
        lanes.append((och >> 3) * 16 + r * 4 + rank)
        zds.append(och & 7)
        rows1.append((row + 1).astype(F32))
    target = jnp.concatenate(targets, axis=1)
    lane = jnp.concatenate(lanes, axis=1)
    zd = jnp.concatenate(zds, axis=1)
    row1 = jnp.concatenate(rows1, axis=1)
    two = NC * DIES_DEV
    left = jnp.where(lax.broadcasted_iota(jnp.int32, (8, two), 0) == zd, row1, 0.0).astype(BF16)
    right = jnp.where(lax.broadcasted_iota(jnp.int32, (128, two), 0) == lane, 1.0, 0.0).astype(BF16)
    table = lax.dot_general(left, right, (((1,), (1,)), ((), ())), preferred_element_type=F32)
    for zz in range(NZ):
        r1snd[zz] = table[zz:zz + 1, :]
    for zz in z_peers:
        send(S_R1, r1snd.at[zz], r1rcv.at[z], dev(y, zz, c, n))
    r1rcv[z] = r1snd[z]
    for l in range(4):
        oh_v[256 * l:256 * l + 256, :] = jnp.where(
            lax.broadcasted_iota(jnp.int32, (256, two), 0) + 256 * l == target, 1.0, 0.0).astype(BF16)

    got(S_M1, m1rcv.at[pl.ds(0, 7)])
    m2snd[...] = jnp.sum(m1rcv[...], axis=0)
    for yy in y_peers:
        send(S_M2, m2snd, m2rcv.at[y], dev(yy, z, c, n))
    m2rcv[y] = m2snd[...]

    got(S_SCORE, arcv.at[pl.ds(0, 7)])
    halves = []
    for cs in range(NC):
        half = (arcv[4 * cs] + arcv[4 * cs + 1]) + (arcv[4 * cs + 2] + arcv[4 * cs + 3])
        halves.append(half)
    s4 = jnp.concatenate([jnp.concatenate([half] * 4, axis=0).T for half in halves], axis=0)
    hi = s4.astype(BF16)
    lo = (s4 - hi.astype(F32)).astype(BF16)
    packed = jnp.dot(oh_v[...], jnp.concatenate([hi, lo], axis=1), preferred_element_type=F32)
    lane_group = lax.broadcasted_iota(jnp.int32, (256, 128), 1) // SLICE
    slots = jnp.zeros((256, 128), F32)
    for l in range(4):
        piece = packed[256 * l:256 * l + 256, :]
        slots = jnp.where(lane_group == l, piece[:, :128] + piece[:, 128:], slots)
    for r in range(4):
        csnd[:, r, :] = slots[64 * r:64 * r + 64, :]
    first = jnp.sum(s4, axis=0, keepdims=True)
    second = jnp.sum(s4 * s4, axis=0, keepdims=True)
    stat = jnp.where(lax.broadcasted_iota(jnp.int32, (1, 128), 1) < SLICE, first, second)
    csnd[:, 4, :] = jnp.broadcast_to(stat, (CHIPS, 128))

    pl.semaphore_wait(plane_sem, len(y_peers))
    order = sorted(range(1, CHIPS), key=lambda j: -(min(j // 8, 8 - j // 8) + min(j % 8, 8 - j % 8)))
    for j in order:
        yy, zz = (y + j // 8) % NY, (z + j % 8) % NZ
        send(S_CHIP, csnd.at[yy * NZ + zz], crcv.at[chip], dev(yy, zz, c, n))
    crcv[chip] = csnd[chip]

    for cs in range(NC):
        bsnd[cs] = halves[cs].astype(BF16)
    for cc, nn in group_peers:
        send(S_BACK, bsnd.at[cc], brcv.at[me8], dev(y, z, cc, nn))
    brcv[me8] = bsnd[c]

    got(S_R1, r1rcv.at[pl.ds(0, 7)])
    here = r1rcv[:, 0, :]
    for yy in range(NY):
        r2snd[yy] = here if yy == 0 else pltpu.roll(here, 128 - 16 * yy, 1)
    for yy in y_peers:
        send(S_R2, r2snd.at[yy], r2rcv.at[y], dev(yy, z, c, n))
    r2rcv[y] = r2snd[y]

    got(S_M2, m2rcv.at[pl.ds(0, 7)])
    m3snd[...] = jnp.sum(m2rcv[...], axis=0)
    send(S_M3, m3snd, m3rcv.at[c], dev(y, z, 1 - c, n))
    m3rcv[c] = m3snd[...]

    got(S_R2, r2rcv.at[pl.ds(0, 7)])
    rr = r2rcv[...].reshape(CHIPS, 128).astype(jnp.int32)
    spot = lax.broadcasted_iota(jnp.int32, (CHIPS, DIES_DEV), 1) + 1
    for cp in range(NC):
        for l in range(4):
            for cs in range(NC):
                s16 = (2 * cp + cs) * 4 + l
                ohr_v[cp, pl.ds(l * 128 + cs * 64, 64), :] = jnp.where(
                    rr[:, s16:s16 + 1] == spot, 1.0, 0.0).astype(BF16)

    got(S_M3, m3rcv.at[0])
    got(S_MET, met_v.at[0])
    both = m3rcv[0] + m3rcv[1]
    center = both[0:4, :] / TOTAL
    scaling = lax.rsqrt(both[4:8, :] / TOTAL - center * center + EPSILON)
    for cs in range(NC):
        for t in range(4):
            span = slice(128 * t, 128 * t + 128)
            mz_v[256 * cs:256 * cs + 256, span] = (
                (met_v[cs, :, span].astype(F32) - center[t:t + 1, :]) * scaling[t:t + 1, :]
            ).astype(BF16)

    got(S_CHIP, crcv.at[pl.ds(0, 63)])
    stat = jnp.sum(crcv[:, 4, :], axis=0, keepdims=True)
    lg = lax.broadcasted_iota(jnp.int32, (1, 128), 1) // SLICE
    s1 = jnp.where(lg == 0, stat, 0.0)
    s2 = jnp.where(lg == 1, stat, 0.0)
    s1 = s1 + pltpu.roll(s1, 32, 1)
    s1 = s1 + pltpu.roll(s1, 64, 1)
    s2 = s2 + pltpu.roll(s2, 32, 1)
    s2 = s2 + pltpu.roll(s2, 64, 1)
    center = s1 / TOTAL
    scaling = lax.rsqrt(s2 / TOTAL - center * center + EPSILON)
    zf = jnp.concatenate([(crcv[:, r, :] - center) * scaling for r in range(4)], axis=0)
    zt = zf.T.astype(BF16)
    for cp in range(NC):
        lhs = jnp.concatenate([zt[32 * l:32 * l + 32, 128 * cp:128 * cp + 128] for l in range(4)], axis=1)
        placed_v[n, :, 256 * cp:256 * cp + 256] = jnp.dot(
            lhs, ohr_v[cp], preferred_element_type=F32).astype(BF16)

    for dn in (2, 1, 3):
        send(S_PLACED, placed_v.at[n], placed_v.at[n], dev(y, z, c, (n + dn) % NX))
    got(S_PLACED, placed_v.at[pl.ds(0, 3)])
    cross = jnp.dot(placed_v[...].reshape(4 * SLICE, NC * DIES_DEV), mz_v[...], preferred_element_type=F32)
    for nn in range(NX):
        for kk in range(2):
            for t in range(4):
                base = 32 * nn + 16 * kk
                dsnd[pl.ds(128 * nn + t * 2 + kk, 16, 8), :] = cross[base:base + 16, 128 * t:128 * t + 128]

    for j in order:
        yy, zz = (y + j // 8) % NY, (z + j % 8) % NZ
        block = pl.ds(pl.multiple_of((yy * NZ + zz) * 8, 8), 8)
        send(S_OUT, dsnd.at[block, :], drcv.at[chip], dev(yy, zz, c, n))
    drcv[chip] = dsnd[pl.ds(pl.multiple_of(chip * 8, 8), 8), :]

    got(S_BACK, brcv.at[pl.ds(0, 7)])
    slot_k = lax.broadcasted_iota(jnp.int32, (COMP, COMP), 1)
    c_of, n_of, kk_of, i_of = slot_k // 128, (slot_k // 32) % 4, (slot_k // 16) % 2, slot_k % 16
    natural = 64 * n_of + 4 * i_of + 2 * c_of + kk_of
    perm = jnp.where(lax.broadcasted_iota(jnp.int32, (COMP, COMP), 0) == natural, 1.0, 0.0).astype(BF16)
    score_t = jnp.dot(perm, brcv[...].reshape(COMP, DIES_DEV), preferred_element_type=F32)
    score = score_t.T.astype(BF16)
    acc = jnp.zeros((DIES_DEV, 128), F32)
    for j in range(CHUNKS):
        span = pl.ds(j * step, step)
        rebuilt = lax.dot_general(
            score, load_v[span, :], (((1,), (1,)), ((), ())), preferred_element_type=F32)
        residue = cen_v[:, span].astype(F32) - rebuilt
        residue = residue * residue
        for t in range(step // 128):
            acc = acc + residue[:, 128 * t:128 * t + 128]
    line = jnp.sum(acc.T, axis=0, keepdims=True) / (FEAT * NX)
    esnd[0:1, :] = line[:, :128]
    esnd[1:2, :] = line[:, 128:]
    for dn in (2, 1, 3):
        send(S_RES, esnd, ercv.at[n], dev(y, z, c, (n + dn) % NX))
    ercv[n] = esnd[...]
    got(S_RES, ercv.at[pl.ds(0, 3)])
    total = (ercv[0] + ercv[1]) + (ercv[2] + ercv[3])
    pick = jnp.where(n >= 2, total[1:2, :], total[0:1, :])
    res_out[...] = jnp.where(n % 2 == 1, pick[:, 64:], pick[:, :64])

    got(S_OUT, drcv.at[pl.ds(0, 63)])
    out = jnp.sum(drcv[...], axis=0) * (1.0 / math.sqrt(TOTAL))
    for t in range(4):
        cross_out[:, 128 * t:128 * t + 128] = out[2 * t:2 * t + 2, :]

    sent(S_SCORE, asnd.at[pl.ds(0, 7)])
    sent(S_ROUTE, route_v.at[0])
    for _ in range(7):
        sent(S_M1, m1snd)
        sent(S_M2, m2snd)
    sent(S_M3, m3snd)
    sent(S_MET, met_v.at[0])
    sent(S_PLACED, placed_v.at[pl.ds(0, 3)])
    sent(S_R1, r1snd.at[pl.ds(0, 7)])
    sent(S_R2, r2snd.at[pl.ds(0, 7)])
    sent(S_CHIP, csnd.at[pl.ds(0, 63)])
    sent(S_BACK, brcv.at[pl.ds(0, 7)])
    sent(S_RES, ercv.at[pl.ds(0, 3)])
    sent(S_OUT, drcv.at[pl.ds(0, 63)])


def shards(iv_curves, mean_curve, loadings, metrology, dest_owner, dest_row):
    any_spec = pl.BlockSpec(memory_space=pl.ANY)
    vmem_spec = pl.BlockSpec(memory_space=pltpu.VMEM)
    scratch = [
        pltpu.VMEM((DIES_DEV, FEAT), BF16),
        pltpu.VMEM((1, FEAT), F32),
        pltpu.VMEM((FEAT, COMP), BF16),
        pltpu.VMEM((DIES_DEV, FEAT), BF16),
        pltpu.VMEM((2, COMP, 128), F32),
        pltpu.VMEM((NC, DIES_DEV, METRO), BF16),
        pltpu.VMEM((NC * DIES_DEV, METRO), BF16),
        pltpu.VMEM((NC, 2, 2, 128), jnp.int32),
        pltpu.VMEM((GROUP, SLICE, DIES_DEV), F32),
        pltpu.VMEM((GROUP, SLICE, DIES_DEV), F32),
        pltpu.VMEM((NC, SLICE, DIES_DEV), BF16),
        pltpu.VMEM((GROUP, SLICE, DIES_DEV), BF16),
        pltpu.VMEM((1024, NC * DIES_DEV), BF16),
        pltpu.VMEM((NC, 512, DIES_DEV), BF16),
        pltpu.VMEM((CHIPS, 5, 128), F32),
        pltpu.VMEM((CHIPS, 5, 128), F32),
        pltpu.VMEM((NX, SLICE, NC * DIES_DEV), BF16),
        pltpu.VMEM((CHIPS * 8, 128), F32),
        pltpu.VMEM((CHIPS, 8, 128), F32),
        pltpu.VMEM((8, 128), F32),
        pltpu.VMEM((NZ, 8, 128), F32),
        pltpu.VMEM((8, 128), F32),
        pltpu.VMEM((NY, 8, 128), F32),
        pltpu.VMEM((8, 128), F32),
        pltpu.VMEM((NC, 8, 128), F32),
        pltpu.VMEM((NZ, 1, 128), F32),
        pltpu.VMEM((NZ, 1, 128), F32),
        pltpu.VMEM((NY, 8, 128), F32),
        pltpu.VMEM((NY, 8, 128), F32),
        pltpu.VMEM((2, 128), F32),
        pltpu.VMEM((NX, 2, 128), F32),
        pltpu.SemaphoreType.DMA((2 * CHUNKS + 4,)),
        pltpu.SemaphoreType.DMA((N_SEM,)),
        pltpu.SemaphoreType.DMA((N_SEM,)),
        pltpu.SemaphoreType.REGULAR,
    ]
    residual, cross = pl.pallas_call(
        body,
        out_shape=(
            jax.ShapeDtypeStruct((1, DIES_DEV // NX), F32),
            jax.ShapeDtypeStruct((2, METRO), F32),
        ),
        in_specs=[any_spec] * 6,
        out_specs=(vmem_spec, vmem_spec),
        scratch_shapes=scratch,
        compiler_params=pltpu.CompilerParams(
            collective_id=1, has_side_effects=True, vmem_limit_bytes=63 * 2**20),
        cost_estimate=pl.CostEstimate(flops=10**9, bytes_accessed=3 * 10**6, transcendentals=0),
    )(
        iv_curves,
        mean_curve.reshape(1, FEAT),
        loadings,
        metrology,
        dest_owner.reshape(2, 128),
        dest_row.reshape(2, 128),
    )
    return residual.reshape(DIES_DEV // NX), cross


def solution(mesh):
    in_specs = (
        P("wide", "narrow"),
        P("narrow"),
        P("narrow", None),
        P("wide", "narrow"),
        P("wide"),
        P("wide"),
    )
    out_specs = (P(("wide", "narrow")), P("wide", "narrow"))
    return jax.shard_map(shards, mesh=mesh, in_specs=in_specs, out_specs=out_specs, check_vma=False)
```

```python
import functools
import math

import jax
import jax.numpy as jnp
from jax import lax
from jax.experimental import pallas as pl
from jax.experimental.pallas import tpu as pltpu
from jax.sharding import PartitionSpec as P

EPSILON = 1e-05
MESH = pl.DeviceIdType.MESH
F32 = jnp.float32
BF16 = jnp.bfloat16

NY, NZ, NC, NX = 8, 8, 2, 4
CHIPS = NY * NZ
GROUP = NC * NX
DIES_DEV = 256
FEAT = 2048
COMP = 256
SLICE = COMP // GROUP
METRO = 512
TOTAL = DIES_DEV * CHIPS * NC
CHUNKS = 4
FAR = (4, 3, 5, 2, 6, 1, 7)
(S_ROUTE, S_SCORE, S_MET, S_M1, S_M2, S_M3, S_R1, S_R2, S_CHIP, S_PLACED, S_BACK, S_RES, S_OUT) = range(13)
N_SEM = 13


def body(
    iv_hbm, mean_hbm, load_hbm, met_hbm, own_hbm, row_hbm,
    res_out, cross_out,
    iv_v, mean_v, load_v, cen_v, pt_v, met_v, mz_v, route_v,
    asnd, arcv, bsnd, brcv, oh_v, ohr_v,
    csnd, crcv, placed_v, dsnd, drcv,
    m1snd, m1rcv, m2snd, m2rcv, m3snd, m3rcv,
    r1snd, r1rcv, r2snd, r2rcv, esnd, ercv,
    ld_sem, ssem, rsem, plane_sem,
):
    w = lax.axis_index("wide")
    n = lax.axis_index("narrow")
    y, z, c = w // 16, (w // 2) % 8, w % 2
    me8 = c * NX + n
    chip = y * NZ + z

    def dev(yy, zz, cc, nn):
        return (yy * 16 + zz * 2 + cc, nn)

    def send(k, src, dst, device):
        pltpu.make_async_remote_copy(
            src_ref=src, dst_ref=dst, send_sem=ssem.at[k], recv_sem=rsem.at[k],
            device_id=device, device_id_type=MESH,
        ).start()

    def got(k, ref):
        pltpu.make_async_copy(ref, ref, rsem.at[k]).wait()

    def sent(k, ref):
        pltpu.make_async_copy(ref, ref, ssem.at[k]).wait()

    group_peers = [((c + dc) % NC, (n + dn) % NX) for dn in (2, 1, 3, 0) for dc in (0, 1) if (dc, dn) != (0, 0)]
    z_peers = [(z + d) % NZ for d in FAR]
    y_peers = [(y + d) % NY for d in FAR]

    step = FEAT // CHUNKS
    loads = []
    for j in range(CHUNKS):
        span = pl.ds(j * step, step)
        loads.append((
            pltpu.make_async_copy(iv_hbm.at[:, span], iv_v.at[:, span], ld_sem.at[2 * j]),
            pltpu.make_async_copy(load_hbm.at[span], load_v.at[span], ld_sem.at[2 * j + 1]),
        ))
    mean_load = pltpu.make_async_copy(mean_hbm, mean_v, ld_sem.at[2 * CHUNKS])
    met_load = pltpu.make_async_copy(met_hbm, met_v.at[c], ld_sem.at[2 * CHUNKS + 1])
    own_load = pltpu.make_async_copy(own_hbm, route_v.at[c, 0], ld_sem.at[2 * CHUNKS + 2])
    row_load = pltpu.make_async_copy(row_hbm, route_v.at[c, 1], ld_sem.at[2 * CHUNKS + 3])
    mean_load.start()
    for a, b in loads:
        a.start()
        b.start()

    barrier = pltpu.get_barrier_semaphore()
    for zz in z_peers:
        pl.semaphore_signal(barrier, inc=1, device_id=dev(y, zz, c, n), device_id_type=MESH)
    for yy in y_peers:
        pl.semaphore_signal(barrier, inc=1, device_id=dev(yy, z, c, n), device_id_type=MESH)
    for cc, nn in group_peers:
        pl.semaphore_signal(barrier, inc=1, device_id=dev(y, z, cc, nn), device_id_type=MESH)

    met_load.start()
    own_load.start()
    row_load.start()

    mean_load.wait()
    part = jnp.zeros((DIES_DEV, COMP), F32)
    for j, (a, b) in enumerate(loads):
        a.wait()
        b.wait()
        span = pl.ds(j * step, step)
        cen = (iv_v[:, span].astype(F32) - mean_v[:, span]).astype(BF16)
        cen_v[:, span] = cen
        part = part + jnp.dot(cen, load_v[span, :], preferred_element_type=F32)
    lead = part[0:1, :].astype(BF16).astype(F32)
    part = jnp.where(lax.broadcasted_iota(jnp.int32, (DIES_DEV, COMP), 0) == 0, lead, part - lead)
    part_t = part.T
    for t in range(2):
        pt_v[t] = part_t[:, 128 * t:128 * t + 128]
    for cc in range(NC):
        for nn in range(NX):
            for kk in range(2):
                for t in range(2):
                    asnd[cc * NX + nn, 16 * kk:16 * kk + 16, 128 * t:128 * t + 128] = pt_v[
                        t, pl.ds(64 * nn + 2 * cc + kk, 16, 4), :].astype(BF16)

    pl.semaphore_wait(barrier, len(z_peers) + len(y_peers) + len(group_peers))

    for cc, nn in group_peers:
        q = cc * NX + nn
        send(S_SCORE, asnd.at[q], arcv.at[me8], dev(y, z, cc, nn))
    for yy in y_peers:
        pl.semaphore_signal(plane_sem, inc=1, device_id=dev(yy, z, c, n), device_id_type=MESH)

    met_load.wait()
    met = met_v[c].astype(F32)
    tot = jnp.sum(met, axis=0, keepdims=True)
    sq = jnp.sum(met * met, axis=0, keepdims=True)
    for t in range(4):
        m1snd[t:t + 1, :] = tot[:, 128 * t:128 * t + 128]
        m1snd[4 + t:5 + t, :] = sq[:, 128 * t:128 * t + 128]
    own_load.wait()
    row_load.wait()

    send(S_ROUTE, route_v.at[c], route_v.at[c], dev(y, z, 1 - c, n))
    for zz in z_peers:
        send(S_M1, m1snd, m1rcv.at[z], dev(y, zz, c, n))
    send(S_MET, met_v.at[c], met_v.at[c], dev(y, z, 1 - c, n))
    arcv[me8] = asnd[me8]
    m1rcv[z] = m1snd[...]

    got(S_ROUTE, route_v.at[0])
    targets, lanes, zds, rows1 = [], [], [], []
    for cs in range(NC):
        owner = jnp.concatenate([route_v[cs, 0, 0:1, :], route_v[cs, 0, 1:2, :]], axis=1)
        row = jnp.concatenate([route_v[cs, 1, 0:1, :], route_v[cs, 1, 1:2, :]], axis=1)
        wide_o = jnp.broadcast_to(owner.astype(F32), (DIES_DEV, DIES_DEV))
        before = lax.broadcasted_iota(jnp.int32, (DIES_DEV, DIES_DEV), 0) < lax.broadcasted_iota(
            jnp.int32, (DIES_DEV, DIES_DEV), 1)
        same = jnp.where((wide_o.T == wide_o) & before, 1.0, 0.0)
        rank = jnp.sum(same, axis=0, keepdims=True).astype(jnp.int32)
        oc = owner & 1
        och = owner >> 1
        r = 2 * oc + cs
        targets.append(rank * 256 + r * 64 + och)
        lanes.append((och >> 3) * 16 + r * 4 + rank)
        zds.append(och & 7)
        rows1.append((row + 1).astype(F32))
    target = jnp.concatenate(targets, axis=1)
    lane = jnp.concatenate(lanes, axis=1)
    zd = jnp.concatenate(zds, axis=1)
    row1 = jnp.concatenate(rows1, axis=1)
    two = NC * DIES_DEV
    left = jnp.where(lax.broadcasted_iota(jnp.int32, (8, two), 0) == zd, row1, 0.0).astype(BF16)
    right = jnp.where(lax.broadcasted_iota(jnp.int32, (128, two), 0) == lane, 1.0, 0.0).astype(BF16)
    table = lax.dot_general(left, right, (((1,), (1,)), ((), ())), preferred_element_type=F32)
    for zz in range(NZ):
        r1snd[zz] = table[zz:zz + 1, :]
    for zz in z_peers:
        send(S_R1, r1snd.at[zz], r1rcv.at[z], dev(y, zz, c, n))
    r1rcv[z] = r1snd[z]
    for l in range(4):
        oh_v[256 * l:256 * l + 256, :] = jnp.where(
            lax.broadcasted_iota(jnp.int32, (256, two), 0) + 256 * l == target, 1.0, 0.0).astype(BF16)

    got(S_M1, m1rcv.at[pl.ds(0, 7)])
    m2snd[...] = jnp.sum(m1rcv[...], axis=0)
    for yy in y_peers:
        send(S_M2, m2snd, m2rcv.at[y], dev(yy, z, c, n))
    m2rcv[y] = m2snd[...]

    got(S_SCORE, arcv.at[pl.ds(0, 7)])
    halves = []
    for cs in range(NC):
        half = (arcv[4 * cs].astype(F32) + arcv[4 * cs + 1].astype(F32)) + (arcv[4 * cs + 2].astype(F32) + arcv[4 * cs + 3].astype(F32))
        lead = jnp.where(lax.broadcasted_iota(jnp.int32, half.shape, 1) == 0, 0.0, half[:, 0:1])
        halves.append(half + lead)
    s4 = jnp.concatenate([jnp.concatenate([half] * 4, axis=0).T for half in halves], axis=0)
    hi = s4.astype(BF16)
    lo = (s4 - hi.astype(F32)).astype(BF16)
    packed = jnp.dot(oh_v[...], jnp.concatenate([hi, lo], axis=1), preferred_element_type=F32)
    lane_group = lax.broadcasted_iota(jnp.int32, (256, 128), 1) // SLICE
    slots = jnp.zeros((256, 128), F32)
    for l in range(4):
        piece = packed[256 * l:256 * l + 256, :]
        slots = jnp.where(lane_group == l, piece[:, :128] + piece[:, 128:], slots)
    for r in range(4):
        csnd[:, r, :] = slots[64 * r:64 * r + 64, :]
    first = jnp.sum(s4, axis=0, keepdims=True)
    second = jnp.sum(s4 * s4, axis=0, keepdims=True)
    stat = jnp.where(lax.broadcasted_iota(jnp.int32, (1, 128), 1) < SLICE, first, second)
    csnd[:, 4, :] = jnp.broadcast_to(stat, (CHIPS, 128))

    pl.semaphore_wait(plane_sem, len(y_peers))
    order = sorted(range(1, CHIPS), key=lambda j: -(min(j // 8, 8 - j // 8) + min(j % 8, 8 - j % 8)))
    for j in order:
        yy, zz = (y + j // 8) % NY, (z + j % 8) % NZ
        send(S_CHIP, csnd.at[yy * NZ + zz], crcv.at[chip], dev(yy, zz, c, n))
    crcv[chip] = csnd[chip]

    for cs in range(NC):
        bsnd[cs] = halves[cs].astype(BF16)
    for cc, nn in group_peers:
        send(S_BACK, bsnd.at[cc], brcv.at[me8], dev(y, z, cc, nn))
    brcv[me8] = bsnd[c]

    got(S_R1, r1rcv.at[pl.ds(0, 7)])
    here = r1rcv[:, 0, :]
    for yy in range(NY):
        r2snd[yy] = here if yy == 0 else pltpu.roll(here, 128 - 16 * yy, 1)
    for yy in y_peers:
        send(S_R2, r2snd.at[yy], r2rcv.at[y], dev(yy, z, c, n))
    r2rcv[y] = r2snd[y]

    got(S_M2, m2rcv.at[pl.ds(0, 7)])
    m3snd[...] = jnp.sum(m2rcv[...], axis=0)
    send(S_M3, m3snd, m3rcv.at[c], dev(y, z, 1 - c, n))
    m3rcv[c] = m3snd[...]

    got(S_R2, r2rcv.at[pl.ds(0, 7)])
    rr = r2rcv[...].reshape(CHIPS, 128).astype(jnp.int32)
    spot = lax.broadcasted_iota(jnp.int32, (CHIPS, DIES_DEV), 1) + 1
    for cp in range(NC):
        for l in range(4):
            for cs in range(NC):
                s16 = (2 * cp + cs) * 4 + l
                ohr_v[cp, pl.ds(l * 128 + cs * 64, 64), :] = jnp.where(
                    rr[:, s16:s16 + 1] == spot, 1.0, 0.0).astype(BF16)

    got(S_M3, m3rcv.at[0])
    got(S_MET, met_v.at[0])
    both = m3rcv[0] + m3rcv[1]
    center = both[0:4, :] / TOTAL
    scaling = lax.rsqrt(both[4:8, :] / TOTAL - center * center + EPSILON)
    for cs in range(NC):
        for t in range(4):
            span = slice(128 * t, 128 * t + 128)
            mz_v[256 * cs:256 * cs + 256, span] = (
                (met_v[cs, :, span].astype(F32) - center[t:t + 1, :]) * scaling[t:t + 1, :]
            ).astype(BF16)

    got(S_CHIP, crcv.at[pl.ds(0, 63)])
    stat = jnp.sum(crcv[:, 4, :], axis=0, keepdims=True)
    lg = lax.broadcasted_iota(jnp.int32, (1, 128), 1) // SLICE
    s1 = jnp.where(lg == 0, stat, 0.0)
    s2 = jnp.where(lg == 1, stat, 0.0)
    s1 = s1 + pltpu.roll(s1, 32, 1)
    s1 = s1 + pltpu.roll(s1, 64, 1)
    s2 = s2 + pltpu.roll(s2, 32, 1)
    s2 = s2 + pltpu.roll(s2, 64, 1)
    center = s1 / TOTAL
    scaling = lax.rsqrt(s2 / TOTAL - center * center + EPSILON)
    zf = jnp.concatenate([(crcv[:, r, :] - center) * scaling for r in range(4)], axis=0)
    zt = zf.T.astype(BF16)
    for cp in range(NC):
        lhs = jnp.concatenate([zt[32 * l:32 * l + 32, 128 * cp:128 * cp + 128] for l in range(4)], axis=1)
        placed_v[n, :, 256 * cp:256 * cp + 256] = jnp.dot(
            lhs, ohr_v[cp], preferred_element_type=F32).astype(BF16)

    for dn in (2, 1, 3):
        send(S_PLACED, placed_v.at[n], placed_v.at[n], dev(y, z, c, (n + dn) % NX))

    got(S_BACK, brcv.at[pl.ds(0, 7)])
    slot_k = lax.broadcasted_iota(jnp.int32, (COMP, COMP), 1)
    c_of, n_of, kk_of, i_of = slot_k // 128, (slot_k // 32) % 4, (slot_k // 16) % 2, slot_k % 16
    natural = 64 * n_of + 4 * i_of + 2 * c_of + kk_of
    perm = jnp.where(lax.broadcasted_iota(jnp.int32, (COMP, COMP), 0) == natural, 1.0, 0.0).astype(BF16)
    score_t = jnp.dot(perm, brcv[...].reshape(COMP, DIES_DEV), preferred_element_type=F32)
    score = score_t.T.astype(BF16)
    acc = jnp.zeros((DIES_DEV, 128), F32)
    for j in range(CHUNKS):
        span = pl.ds(j * step, step)
        rebuilt = lax.dot_general(
            score, load_v[span, :], (((1,), (1,)), ((), ())), preferred_element_type=F32)
        residue = cen_v[:, span].astype(F32) - rebuilt
        residue = residue * residue
        for t in range(step // 128):
            acc = acc + residue[:, 128 * t:128 * t + 128]
    line = jnp.sum(acc.T, axis=0, keepdims=True) / (FEAT * NX)
    esnd[0:1, :] = line[:, :128]
    esnd[1:2, :] = line[:, 128:]
    for dn in (2, 1, 3):
        send(S_RES, esnd, ercv.at[n], dev(y, z, c, (n + dn) % NX))
    ercv[n] = esnd[...]

    got(S_PLACED, placed_v.at[pl.ds(0, 3)])
    cross = jnp.dot(placed_v[...].reshape(4 * SLICE, NC * DIES_DEV), mz_v[...], preferred_element_type=F32)
    for nn in range(NX):
        for kk in range(2):
            for t in range(4):
                base = 32 * nn + 16 * kk
                dsnd[pl.ds(128 * nn + t * 2 + kk, 16, 8), :] = cross[base:base + 16, 128 * t:128 * t + 128]

    for zz in range(NZ):
        for dy in (0, 1, 7, 2, 6, 3, 5, 4):
            yy = dy
            block = pl.ds(pl.multiple_of((yy * NZ + zz) * 8, 8), 8)

            @pl.when(chip != yy * NZ + zz)
            def _(block=block, yy=yy, zz=zz):
                send(S_OUT, dsnd.at[block, :], drcv.at[chip], dev(yy, zz, c, n))

    drcv[chip] = dsnd[pl.ds(pl.multiple_of(chip * 8, 8), 8), :]

    got(S_RES, ercv.at[pl.ds(0, 3)])
    total = (ercv[0] + ercv[1]) + (ercv[2] + ercv[3])
    pick = jnp.where(n >= 2, total[1:2, :], total[0:1, :])
    res_out[...] = jnp.where(n % 2 == 1, pick[:, 64:], pick[:, :64])

    got(S_OUT, drcv.at[pl.ds(0, 63)])
    out = jnp.sum(drcv[...], axis=0) * (1.0 / math.sqrt(TOTAL))
    for t in range(4):
        cross_out[:, 128 * t:128 * t + 128] = out[2 * t:2 * t + 2, :]

    sent(S_SCORE, asnd.at[pl.ds(0, 7)])
    sent(S_ROUTE, route_v.at[0])
    for _ in range(7):
        sent(S_M1, m1snd)
        sent(S_M2, m2snd)
    sent(S_M3, m3snd)
    sent(S_MET, met_v.at[0])
    sent(S_PLACED, placed_v.at[pl.ds(0, 3)])
    sent(S_R1, r1snd.at[pl.ds(0, 7)])
    sent(S_R2, r2snd.at[pl.ds(0, 7)])
    sent(S_CHIP, csnd.at[pl.ds(0, 63)])
    sent(S_BACK, brcv.at[pl.ds(0, 7)])
    sent(S_RES, ercv.at[pl.ds(0, 3)])
    sent(S_OUT, drcv.at[pl.ds(0, 63)])


def finish(a_ref, b_ref, res_out, cross_out, sem):
    one = pltpu.make_async_copy(a_ref, res_out, sem.at[0])
    two = pltpu.make_async_copy(b_ref, cross_out, sem.at[1])
    one.start()
    two.start()
    one.wait()
    two.wait()


def shards(iv_curves, mean_curve, loadings, metrology, dest_owner, dest_row):
    hbm_spec = pl.BlockSpec(memory_space=pltpu.HBM)
    vmem_spec = pl.BlockSpec(memory_space=pltpu.VMEM)
    scratch = [
        pltpu.VMEM((DIES_DEV, FEAT), BF16),
        pltpu.VMEM((1, FEAT), F32),
        pltpu.VMEM((FEAT, COMP), BF16),
        pltpu.VMEM((DIES_DEV, FEAT), BF16),
        pltpu.VMEM((2, COMP, 128), F32),
        pltpu.VMEM((NC, DIES_DEV, METRO), BF16),
        pltpu.VMEM((NC * DIES_DEV, METRO), BF16),
        pltpu.VMEM((NC, 2, 2, 128), jnp.int32),
        pltpu.VMEM((GROUP, SLICE, DIES_DEV), BF16),
        pltpu.VMEM((GROUP, SLICE, DIES_DEV), BF16),
        pltpu.VMEM((NC, SLICE, DIES_DEV), BF16),
        pltpu.VMEM((GROUP, SLICE, DIES_DEV), BF16),
        pltpu.VMEM((1024, NC * DIES_DEV), BF16),
        pltpu.VMEM((NC, 512, DIES_DEV), BF16),
        pltpu.VMEM((CHIPS, 5, 128), F32),
        pltpu.VMEM((CHIPS, 5, 128), F32),
        pltpu.VMEM((NX, SLICE, NC * DIES_DEV), BF16),
        pltpu.VMEM((CHIPS * 8, 128), F32),
        pltpu.VMEM((CHIPS, 8, 128), F32),
        pltpu.VMEM((8, 128), F32),
        pltpu.VMEM((NZ, 8, 128), F32),
        pltpu.VMEM((8, 128), F32),
        pltpu.VMEM((NY, 8, 128), F32),
        pltpu.VMEM((8, 128), F32),
        pltpu.VMEM((NC, 8, 128), F32),
        pltpu.VMEM((NZ, 1, 128), F32),
        pltpu.VMEM((NZ, 1, 128), F32),
        pltpu.VMEM((NY, 8, 128), F32),
        pltpu.VMEM((NY, 8, 128), F32),
        pltpu.VMEM((2, 128), F32),
        pltpu.VMEM((NX, 2, 128), F32),
        pltpu.SemaphoreType.DMA((2 * CHUNKS + 4,)),
        pltpu.SemaphoreType.DMA((N_SEM,)),
        pltpu.SemaphoreType.DMA((N_SEM,)),
        pltpu.SemaphoreType.REGULAR,
    ]
    residual, cross = pl.pallas_call(
        body,
        out_shape=(
            jax.ShapeDtypeStruct((1, DIES_DEV // NX), F32),
            jax.ShapeDtypeStruct((2, METRO), F32),
        ),
        in_specs=[hbm_spec] * 6,
        out_specs=(vmem_spec, vmem_spec),
        scratch_shapes=scratch,
        compiler_params=pltpu.CompilerParams(
            collective_id=1, has_side_effects=True, vmem_limit_bytes=63 * 2**20),
        cost_estimate=pl.CostEstimate(flops=10**9, bytes_accessed=3 * 10**6, transcendentals=0),
    )(
        iv_curves,
        mean_curve.reshape(1, FEAT),
        loadings,
        metrology,
        dest_owner.reshape(2, 128),
        dest_row.reshape(2, 128),
    )
    any_spec = pl.BlockSpec(memory_space=pl.ANY)
    residual, cross = pl.pallas_call(
        finish,
        out_shape=(
            jax.ShapeDtypeStruct((1, DIES_DEV // NX), F32),
            jax.ShapeDtypeStruct((2, METRO), F32),
        ),
        in_specs=[any_spec, any_spec],
        out_specs=(any_spec, any_spec),
        scratch_shapes=[pltpu.SemaphoreType.DMA((2,))],
    )(residual, cross)
    return residual.reshape(DIES_DEV // NX), cross


def solution(mesh):
    in_specs = (
        P("wide", "narrow"),
        P("narrow"),
        P("narrow", None),
        P("wide", "narrow"),
        P("wide"),
        P("wide"),
    )
    out_specs = (P(("wide", "narrow")), P("wide", "narrow"))
    return jax.shard_map(shards, mesh=mesh, in_specs=in_specs, out_specs=out_specs, check_vma=False)
```

```python
import functools
import math

import jax
import jax.numpy as jnp
from jax import lax
from jax.experimental import pallas as pl
from jax.experimental.pallas import tpu as pltpu
from jax.sharding import PartitionSpec as P

EPSILON = 1e-05
MESH = pl.DeviceIdType.MESH
F32 = jnp.float32
BF16 = jnp.bfloat16

NY, NZ, NC, NX = 8, 8, 2, 4
CHIPS = NY * NZ
GROUP = NC * NX
DIES_DEV = 256
FEAT = 2048
COMP = 256
SLICE = COMP // GROUP
METRO = 512
TOTAL = DIES_DEV * CHIPS * NC
CHUNKS = 4
FAR = (4, 3, 5, 2, 6, 1, 7)
(S_ROUTE, S_SCORE, S_MET, S_M1, S_M2, S_M3, S_R1, S_R2, S_CHIP, S_PLACED, S_BACK, S_RES, S_OUT) = range(13)
N_SEM = 13


def body(
    iv_hbm, mean_hbm, load_hbm, met_hbm, own_hbm, row_hbm,
    res_out, cross_out,
    iv_v, mean_v, load_v, cen_v, pt_v, met_v, mz_v, route_v,
    asnd, arcv, bsnd, brcv, oh_v, ohr_v,
    csnd, crcv, placed_v, dsnd, drcv,
    m1snd, m1rcv, m2snd, m2rcv, m3snd, m3rcv,
    r1snd, r1rcv, r2snd, r2rcv, esnd, ercv,
    ld_sem, ssem, rsem, plane_sem,
):
    w = lax.axis_index("wide")
    n = lax.axis_index("narrow")
    y, z, c = w // 16, (w // 2) % 8, w % 2
    me8 = c * NX + n
    chip = y * NZ + z

    def dev(yy, zz, cc, nn):
        return (yy * 16 + zz * 2 + cc, nn)

    def send(k, src, dst, device):
        pltpu.make_async_remote_copy(
            src_ref=src, dst_ref=dst, send_sem=ssem.at[k], recv_sem=rsem.at[k],
            device_id=device, device_id_type=MESH,
        ).start()

    def got(k, ref):
        pltpu.make_async_copy(ref, ref, rsem.at[k]).wait()

    def sent(k, ref):
        pltpu.make_async_copy(ref, ref, ssem.at[k]).wait()

    group_peers = [((c + dc) % NC, (n + dn) % NX) for dn in (2, 1, 3, 0) for dc in (0, 1) if (dc, dn) != (0, 0)]
    z_peers = [(z + d) % NZ for d in FAR]
    y_peers = [(y + d) % NY for d in FAR]

    step = FEAT // CHUNKS
    loads = []
    for j in range(CHUNKS):
        span = pl.ds(j * step, step)
        loads.append((
            pltpu.make_async_copy(iv_hbm.at[:, span], iv_v.at[:, span], ld_sem.at[2 * j]),
            pltpu.make_async_copy(load_hbm.at[span], load_v.at[span], ld_sem.at[2 * j + 1]),
        ))
    mean_load = pltpu.make_async_copy(mean_hbm, mean_v, ld_sem.at[2 * CHUNKS])
    met_load = pltpu.make_async_copy(met_hbm, met_v.at[c], ld_sem.at[2 * CHUNKS + 1])
    own_load = pltpu.make_async_copy(own_hbm, route_v.at[c, 0], ld_sem.at[2 * CHUNKS + 2])
    row_load = pltpu.make_async_copy(row_hbm, route_v.at[c, 1], ld_sem.at[2 * CHUNKS + 3])
    met_load.start()
    mean_load.start()
    for a, b in loads:
        a.start()
        b.start()
    own_load.start()
    row_load.start()

    barrier = pltpu.get_barrier_semaphore()
    for zz in z_peers:
        pl.semaphore_signal(barrier, inc=1, device_id=dev(y, zz, c, n), device_id_type=MESH)
    for yy in y_peers:
        pl.semaphore_signal(barrier, inc=1, device_id=dev(yy, z, c, n), device_id_type=MESH)
    for cc, nn in group_peers:
        pl.semaphore_signal(barrier, inc=1, device_id=dev(y, z, cc, nn), device_id_type=MESH)

    met_load.wait()
    met = met_v[c].astype(F32)
    tot = jnp.sum(met, axis=0, keepdims=True)
    sq = jnp.sum(met * met, axis=0, keepdims=True)
    for t in range(4):
        m1snd[t:t + 1, :] = tot[:, 128 * t:128 * t + 128]
        m1snd[4 + t:5 + t, :] = sq[:, 128 * t:128 * t + 128]

    mean_load.wait()
    part = jnp.zeros((DIES_DEV, COMP), F32)
    for j, (a, b) in enumerate(loads):
        a.wait()
        b.wait()
        span = pl.ds(j * step, step)
        cen = (iv_v[:, span].astype(F32) - mean_v[:, span]).astype(BF16)
        cen_v[:, span] = cen
        part = part + jnp.dot(cen, load_v[span, :], preferred_element_type=F32)
    lead = part[0:1, :].astype(BF16).astype(F32)
    part = jnp.where(lax.broadcasted_iota(jnp.int32, (DIES_DEV, COMP), 0) == 0, lead, part - lead)
    part_t = part.T
    for t in range(2):
        pt_v[t] = part_t[:, 128 * t:128 * t + 128]
    for cc in range(NC):
        for nn in range(NX):
            for kk in range(2):
                for t in range(2):
                    asnd[cc * NX + nn, 16 * kk:16 * kk + 16, 128 * t:128 * t + 128] = pt_v[
                        t, pl.ds(64 * nn + 2 * cc + kk, 16, 4), :].astype(BF16)

    pl.semaphore_wait(barrier, len(z_peers) + len(y_peers) + len(group_peers))

    for cc, nn in group_peers:
        q = cc * NX + nn
        send(S_SCORE, asnd.at[q], arcv.at[me8], dev(y, z, cc, nn))
    for zz in z_peers:
        send(S_M1, m1snd, m1rcv.at[z], dev(y, zz, c, n))
    for yy in y_peers:
        pl.semaphore_signal(plane_sem, inc=1, device_id=dev(yy, z, c, n), device_id_type=MESH)

    own_load.wait()
    row_load.wait()
    send(S_ROUTE, route_v.at[c], route_v.at[c], dev(y, z, 1 - c, n))
    send(S_MET, met_v.at[c], met_v.at[c], dev(y, z, 1 - c, n))
    arcv[me8] = asnd[me8]
    m1rcv[z] = m1snd[...]

    got(S_ROUTE, route_v.at[0])
    targets, lanes, zds, rows1 = [], [], [], []
    for cs in range(NC):
        owner = jnp.concatenate([route_v[cs, 0, 0:1, :], route_v[cs, 0, 1:2, :]], axis=1)
        row = jnp.concatenate([route_v[cs, 1, 0:1, :], route_v[cs, 1, 1:2, :]], axis=1)
        wide_o = jnp.broadcast_to(owner.astype(F32), (DIES_DEV, DIES_DEV))
        before = lax.broadcasted_iota(jnp.int32, (DIES_DEV, DIES_DEV), 0) < lax.broadcasted_iota(
            jnp.int32, (DIES_DEV, DIES_DEV), 1)
        same = jnp.where((wide_o.T == wide_o) & before, 1.0, 0.0)
        rank = jnp.sum(same, axis=0, keepdims=True).astype(jnp.int32)
        oc = owner & 1
        och = owner >> 1
        r = 2 * oc + cs
        targets.append(rank * 256 + r * 64 + och)
        lanes.append((och >> 3) * 16 + r * 4 + rank)
        zds.append(och & 7)
        rows1.append((row + 1).astype(F32))
    target = jnp.concatenate(targets, axis=1)
    lane = jnp.concatenate(lanes, axis=1)
    zd = jnp.concatenate(zds, axis=1)
    row1 = jnp.concatenate(rows1, axis=1)
    two = NC * DIES_DEV
    left = jnp.where(lax.broadcasted_iota(jnp.int32, (8, two), 0) == zd, row1, 0.0).astype(BF16)
    right = jnp.where(lax.broadcasted_iota(jnp.int32, (128, two), 0) == lane, 1.0, 0.0).astype(BF16)
    table = lax.dot_general(left, right, (((1,), (1,)), ((), ())), preferred_element_type=F32)
    for zz in range(NZ):
        r1snd[zz] = table[zz:zz + 1, :]
    for zz in z_peers:
        send(S_R1, r1snd.at[zz], r1rcv.at[z], dev(y, zz, c, n))
    r1rcv[z] = r1snd[z]
    for l in range(4):
        oh_v[256 * l:256 * l + 256, :] = jnp.where(
            lax.broadcasted_iota(jnp.int32, (256, two), 0) + 256 * l == target, 1.0, 0.0).astype(BF16)

    got(S_SCORE, arcv.at[pl.ds(0, 7)])
    halves = []
    for cs in range(NC):
        half = (arcv[4 * cs].astype(F32) + arcv[4 * cs + 1].astype(F32)) + (arcv[4 * cs + 2].astype(F32) + arcv[4 * cs + 3].astype(F32))
        lead = jnp.where(lax.broadcasted_iota(jnp.int32, half.shape, 1) == 0, 0.0, half[:, 0:1])
        halves.append(half + lead)
    s4 = jnp.concatenate([jnp.concatenate([half] * 4, axis=0).T for half in halves], axis=0)
    hi = s4.astype(BF16)
    lo = (s4 - hi.astype(F32)).astype(BF16)
    packed = jnp.dot(oh_v[...], jnp.concatenate([hi, lo], axis=1), preferred_element_type=F32)
    lane_group = lax.broadcasted_iota(jnp.int32, (256, 128), 1) // SLICE
    slots = jnp.zeros((256, 128), F32)
    for l in range(4):
        piece = packed[256 * l:256 * l + 256, :]
        slots = jnp.where(lane_group == l, piece[:, :128] + piece[:, 128:], slots)
    for r in range(4):
        csnd[:, r, :] = slots[64 * r:64 * r + 64, :]
    first = jnp.sum(s4, axis=0, keepdims=True)
    second = jnp.sum(s4 * s4, axis=0, keepdims=True)
    stat = jnp.where(lax.broadcasted_iota(jnp.int32, (1, 128), 1) < SLICE, first, second)
    csnd[:, 4, :] = jnp.broadcast_to(stat, (CHIPS, 128))

    pl.semaphore_wait(plane_sem, len(y_peers))
    got(S_M1, m1rcv.at[pl.ds(0, 7)])
    m2snd[...] = jnp.sum(m1rcv[...], axis=0)
    for yy in y_peers:
        send(S_M2, m2snd, m2rcv.at[y], dev(yy, z, c, n))
    m2rcv[y] = m2snd[...]

    order = sorted(range(1, CHIPS), key=lambda j: -(min(j // 8, 8 - j // 8) + min(j % 8, 8 - j % 8)))
    for j in order:
        yy, zz = (y + j // 8) % NY, (z + j % 8) % NZ
        send(S_CHIP, csnd.at[yy * NZ + zz], crcv.at[chip], dev(yy, zz, c, n))
    crcv[chip] = csnd[chip]

    for cs in range(NC):
        bsnd[cs] = halves[cs].astype(BF16)
    for cc, nn in group_peers:
        send(S_BACK, bsnd.at[cc], brcv.at[me8], dev(y, z, cc, nn))
    brcv[me8] = bsnd[c]

    got(S_R1, r1rcv.at[pl.ds(0, 7)])
    here = r1rcv[:, 0, :]
    for yy in range(NY):
        r2snd[yy] = here if yy == 0 else pltpu.roll(here, 128 - 16 * yy, 1)
    for yy in y_peers:
        send(S_R2, r2snd.at[yy], r2rcv.at[y], dev(yy, z, c, n))
    r2rcv[y] = r2snd[y]

    got(S_M2, m2rcv.at[pl.ds(0, 7)])
    m3snd[...] = jnp.sum(m2rcv[...], axis=0)
    send(S_M3, m3snd, m3rcv.at[c], dev(y, z, 1 - c, n))
    m3rcv[c] = m3snd[...]

    got(S_R2, r2rcv.at[pl.ds(0, 7)])
    rr = r2rcv[...].reshape(CHIPS, 128).astype(jnp.int32)
    spot = lax.broadcasted_iota(jnp.int32, (CHIPS, DIES_DEV), 1) + 1
    for cp in range(NC):
        for l in range(4):
            for cs in range(NC):
                s16 = (2 * cp + cs) * 4 + l
                ohr_v[cp, pl.ds(l * 128 + cs * 64, 64), :] = jnp.where(
                    rr[:, s16:s16 + 1] == spot, 1.0, 0.0).astype(BF16)

    got(S_CHIP, crcv.at[pl.ds(0, 63)])
    stat = jnp.sum(crcv[:, 4, :], axis=0, keepdims=True)
    lg = lax.broadcasted_iota(jnp.int32, (1, 128), 1) // SLICE
    s1 = jnp.where(lg == 0, stat, 0.0)
    s2 = jnp.where(lg == 1, stat, 0.0)
    s1 = s1 + pltpu.roll(s1, 32, 1)
    s1 = s1 + pltpu.roll(s1, 64, 1)
    s2 = s2 + pltpu.roll(s2, 32, 1)
    s2 = s2 + pltpu.roll(s2, 64, 1)
    center = s1 / TOTAL
    scaling = lax.rsqrt(s2 / TOTAL - center * center + EPSILON)
    zf = jnp.concatenate([(crcv[:, r, :] - center) * scaling for r in range(4)], axis=0)
    zt = zf.T.astype(BF16)
    for cp in range(NC):
        lhs = jnp.concatenate([zt[32 * l:32 * l + 32, 128 * cp:128 * cp + 128] for l in range(4)], axis=1)
        placed_v[n, :, 256 * cp:256 * cp + 256] = jnp.dot(
            lhs, ohr_v[cp], preferred_element_type=F32).astype(BF16)

    for dn in (2, 1, 3):
        send(S_PLACED, placed_v.at[n], placed_v.at[n], dev(y, z, c, (n + dn) % NX))

    got(S_M3, m3rcv.at[0])
    got(S_MET, met_v.at[0])
    both = m3rcv[0] + m3rcv[1]
    center = both[0:4, :] / TOTAL
    scaling = lax.rsqrt(both[4:8, :] / TOTAL - center * center + EPSILON)
    for cs in range(NC):
        for t in range(4):
            span = slice(128 * t, 128 * t + 128)
            mz_v[256 * cs:256 * cs + 256, span] = (
                (met_v[cs, :, span].astype(F32) - center[t:t + 1, :]) * scaling[t:t + 1, :]
            ).astype(BF16)

    got(S_BACK, brcv.at[pl.ds(0, 7)])
    slot_k = lax.broadcasted_iota(jnp.int32, (COMP, COMP), 1)
    c_of, n_of, kk_of, i_of = slot_k // 128, (slot_k // 32) % 4, (slot_k // 16) % 2, slot_k % 16
    natural = 64 * n_of + 4 * i_of + 2 * c_of + kk_of
    perm = jnp.where(lax.broadcasted_iota(jnp.int32, (COMP, COMP), 0) == natural, 1.0, 0.0).astype(BF16)
    score_t = jnp.dot(perm, brcv[...].reshape(COMP, DIES_DEV), preferred_element_type=F32)
    score = score_t.T.astype(BF16)
    acc = jnp.zeros((DIES_DEV, 128), F32)
    for j in range(CHUNKS):
        span = pl.ds(j * step, step)
        rebuilt = lax.dot_general(
            score, load_v[span, :], (((1,), (1,)), ((), ())), preferred_element_type=F32)
        residue = cen_v[:, span].astype(F32) - rebuilt
        residue = residue * residue
        for t in range(step // 128):
            acc = acc + residue[:, 128 * t:128 * t + 128]
    line = jnp.sum(acc.T, axis=0, keepdims=True) / (FEAT * NX)
    esnd[0:1, :] = line[:, :128]
    esnd[1:2, :] = line[:, 128:]
    for dn in (2, 1, 3):
        send(S_RES, esnd, ercv.at[n], dev(y, z, c, (n + dn) % NX))
    ercv[n] = esnd[...]

    got(S_PLACED, placed_v.at[pl.ds(0, 3)])
    cross = jnp.dot(placed_v[...].reshape(4 * SLICE, NC * DIES_DEV), mz_v[...], preferred_element_type=F32)
    for nn in range(NX):
        for kk in range(2):
            for t in range(4):
                base = 32 * nn + 16 * kk
                dsnd[pl.ds(128 * nn + t * 2 + kk, 16, 8), :] = cross[base:base + 16, 128 * t:128 * t + 128]

    for zz in range(NZ):
        for dy in (0, 1, 7, 2, 6, 3, 5, 4):
            yy = dy
            block = pl.ds(pl.multiple_of((yy * NZ + zz) * 8, 8), 8)

            @pl.when(chip != yy * NZ + zz)
            def _(block=block, yy=yy, zz=zz):
                send(S_OUT, dsnd.at[block, :], drcv.at[chip], dev(yy, zz, c, n))

    drcv[chip] = dsnd[pl.ds(pl.multiple_of(chip * 8, 8), 8), :]

    got(S_RES, ercv.at[pl.ds(0, 3)])
    total = (ercv[0] + ercv[1]) + (ercv[2] + ercv[3])
    pick = jnp.where(n >= 2, total[1:2, :], total[0:1, :])
    res_out[...] = jnp.where(n % 2 == 1, pick[:, 64:], pick[:, :64])

    got(S_OUT, drcv.at[pl.ds(0, 63)])
    out = jnp.sum(drcv[...], axis=0) * (1.0 / math.sqrt(TOTAL))
    for t in range(4):
        cross_out[:, 128 * t:128 * t + 128] = out[2 * t:2 * t + 2, :]

    sent(S_SCORE, asnd.at[pl.ds(0, 7)])
    sent(S_ROUTE, route_v.at[0])
    for _ in range(7):
        sent(S_M1, m1snd)
        sent(S_M2, m2snd)
    sent(S_M3, m3snd)
    sent(S_MET, met_v.at[0])
    sent(S_PLACED, placed_v.at[pl.ds(0, 3)])
    sent(S_R1, r1snd.at[pl.ds(0, 7)])
    sent(S_R2, r2snd.at[pl.ds(0, 7)])
    sent(S_CHIP, csnd.at[pl.ds(0, 63)])
    sent(S_BACK, brcv.at[pl.ds(0, 7)])
    sent(S_RES, ercv.at[pl.ds(0, 3)])
    sent(S_OUT, drcv.at[pl.ds(0, 63)])


def finish(a_ref, b_ref, res_out, cross_out, sem):
    one = pltpu.make_async_copy(a_ref, res_out, sem.at[0])
    two = pltpu.make_async_copy(b_ref, cross_out, sem.at[1])
    one.start()
    two.start()
    one.wait()
    two.wait()


def shards(iv_curves, mean_curve, loadings, metrology, dest_owner, dest_row):
    hbm_spec = pl.BlockSpec(memory_space=pltpu.HBM)
    vmem_spec = pl.BlockSpec(memory_space=pltpu.VMEM)
    scratch = [
        pltpu.VMEM((DIES_DEV, FEAT), BF16),
        pltpu.VMEM((1, FEAT), F32),
        pltpu.VMEM((FEAT, COMP), BF16),
        pltpu.VMEM((DIES_DEV, FEAT), BF16),
        pltpu.VMEM((2, COMP, 128), F32),
        pltpu.VMEM((NC, DIES_DEV, METRO), BF16),
        pltpu.VMEM((NC * DIES_DEV, METRO), BF16),
        pltpu.VMEM((NC, 2, 2, 128), jnp.int32),
        pltpu.VMEM((GROUP, SLICE, DIES_DEV), BF16),
        pltpu.VMEM((GROUP, SLICE, DIES_DEV), BF16),
        pltpu.VMEM((NC, SLICE, DIES_DEV), BF16),
        pltpu.VMEM((GROUP, SLICE, DIES_DEV), BF16),
        pltpu.VMEM((1024, NC * DIES_DEV), BF16),
        pltpu.VMEM((NC, 512, DIES_DEV), BF16),
        pltpu.VMEM((CHIPS, 5, 128), F32),
        pltpu.VMEM((CHIPS, 5, 128), F32),
        pltpu.VMEM((NX, SLICE, NC * DIES_DEV), BF16),
        pltpu.VMEM((CHIPS * 8, 128), F32),
        pltpu.VMEM((CHIPS, 8, 128), F32),
        pltpu.VMEM((8, 128), F32),
        pltpu.VMEM((NZ, 8, 128), F32),
        pltpu.VMEM((8, 128), F32),
        pltpu.VMEM((NY, 8, 128), F32),
        pltpu.VMEM((8, 128), F32),
        pltpu.VMEM((NC, 8, 128), F32),
        pltpu.VMEM((NZ, 1, 128), F32),
        pltpu.VMEM((NZ, 1, 128), F32),
        pltpu.VMEM((NY, 8, 128), F32),
        pltpu.VMEM((NY, 8, 128), F32),
        pltpu.VMEM((2, 128), F32),
        pltpu.VMEM((NX, 2, 128), F32),
        pltpu.SemaphoreType.DMA((2 * CHUNKS + 4,)),
        pltpu.SemaphoreType.DMA((N_SEM,)),
        pltpu.SemaphoreType.DMA((N_SEM,)),
        pltpu.SemaphoreType.REGULAR,
    ]
    residual, cross = pl.pallas_call(
        body,
        out_shape=(
            jax.ShapeDtypeStruct((1, DIES_DEV // NX), F32),
            jax.ShapeDtypeStruct((2, METRO), F32),
        ),
        in_specs=[hbm_spec] * 6,
        out_specs=(vmem_spec, vmem_spec),
        scratch_shapes=scratch,
        compiler_params=pltpu.CompilerParams(
            collective_id=1, has_side_effects=True, vmem_limit_bytes=63 * 2**20),
        cost_estimate=pl.CostEstimate(flops=10**9, bytes_accessed=3 * 10**6, transcendentals=0),
    )(
        iv_curves,
        mean_curve.reshape(1, FEAT),
        loadings,
        metrology,
        dest_owner.reshape(2, 128),
        dest_row.reshape(2, 128),
    )
    any_spec = pl.BlockSpec(memory_space=pl.ANY)
    residual, cross = pl.pallas_call(
        finish,
        out_shape=(
            jax.ShapeDtypeStruct((1, DIES_DEV // NX), F32),
            jax.ShapeDtypeStruct((2, METRO), F32),
        ),
        in_specs=[any_spec, any_spec],
        out_specs=(any_spec, any_spec),
        scratch_shapes=[pltpu.SemaphoreType.DMA((2,))],
    )(residual, cross)
    return residual.reshape(DIES_DEV // NX), cross


def solution(mesh):
    in_specs = (
        P("wide", "narrow"),
        P("narrow"),
        P("narrow", None),
        P("wide", "narrow"),
        P("wide"),
        P("wide"),
    )
    out_specs = (P(("wide", "narrow")), P("wide", "narrow"))
    return jax.shard_map(shards, mesh=mesh, in_specs=in_specs, out_specs=out_specs, check_vma=False)
```
